32 devices in a mesh: rep: 2 (over x), seq: 16 (over z, y, core).
Axes of the slice: x: 2, y: 2, z: 4, core: 2. Of those that a mesh axis runs over, the one named last changes fastest.
Arguments:
- prompt_latent: bfloat16 [32, 2048, 512], P(('rep', 'seq')), parts along dimension 0, may hold values from -6 to 6
- prompt_rope: bfloat16 [32, 64, 2048], P(('rep', 'seq')), parts along dimension 0, may hold values from -8 to 8
- private_latent: bfloat16 [512, 128, 512], P(('rep', 'seq')), parts along dimension 0, may hold values from -6 to 6
- private_rope: bfloat16 [512, 64, 128], P(('rep', 'seq')), parts along dimension 0, may hold values from -6 to 6
- lengths: int32 [512], P(('rep', 'seq')), parts along dimension 0, may hold values from 1 to 128
- survived: int32 [512], P(('rep', 'seq')), parts along dimension 0, may hold values from 0 to 1
- prompt_of: int32 [512], P(('rep', 'seq')), parts along dimension 0, may hold values from 0 to 15, as said below
- new_slot: int32 [512], P(('rep', 'seq')), parts along dimension 0, may hold values from -1 to 255, as said below
- queries: bfloat16 [512, 2, 64, 576], P(('rep', 'seq')), parts along dimension 0, may hold values from -160 to 160
- new_keys: bfloat16 [512, 2, 576], P(('rep', 'seq')), parts along dimension 0, may hold values from -9 to 9
Outputs:
- attention: bfloat16 [512, 2, 64, 512], P(('rep', 'seq')), parts along dimension 0
The draws below stay inside these ranges and needn't reach their ends.
There are 2 independent parts, one for each index of `rep`. The reference program is written for one: setup_inputs(seed, part) draws one part's arguments, and reference() takes and returns one part's arrays. A program takes and returns all parts, laid end to end along the dimension named above; each array names one. Nothing has to cross between parts.
Inputs may be any that keep to these rules, and one draw needn't show every extreme that they name: `prompt_of`: continuation rows d * 16 to (d + 1) * 16 - 1 belong to prompt d or prompt d - 1 (cyclically over the 16 prompts), 8 to each, so every prompt has 16 continuations. -1 exactly where survived is 0; distinct for distinct survivors; the slot's device new_slot // 16 lies within 2 devices of the continuation's own device (c // 16), cyclically; at most 2 survivors of one device go to any one other device, and some device sends exactly 2 to each device within 2.
All inputs are finite; a program needn't handle non-finite values.
Results may differ from the reference program's by a relative error of at most 0.0034.
Values may be sent and summed in bfloat16 or wider, within the bound.
A program may use at most 128 MiB of HBM per device.

```python
import jax
import jax.numpy as jnp
from jax import lax

NH = 64
DC = 512
DR = 64
NOPE = 128
SIBLING_COUNT = 16
STEPS = 2
REACH = 2
BLK = 128
PLEN = 2048
HOMEBOUND_LIMIT = 8
TRANSFER_LIMIT = 2
PROMPTS = 16
CONT = 256


def route_tables(key):
    starting_index = jax.random.fold_in(key, 101)
    processor_count = CONT // SIBLING_COUNT
    random_seeds = jax.random.split(jax.random.fold_in(starting_index, 1), processor_count)
    persisting_order_matrix = jax.vmap(lambda solitary_entry: jax.random.permutation(solitary_entry, SIBLING_COUNT))(random_seeds).astype(jnp.int32)
    persisting_entries = jax.random.randint(jax.random.fold_in(starting_index, 2), (processor_count,), HOMEBOUND_LIMIT - 2, SIBLING_COUNT + 1).astype(jnp.int32)
    centre = jax.random.randint(jax.random.fold_in(starting_index, 3), (), 0, processor_count).astype(jnp.int32)
    device_ids = jnp.arange(processor_count, dtype=jnp.int32)
    distance = (device_ids - centre) % processor_count
    neighbour_markers = (distance >= 1) & (distance <= REACH) | (distance >= processor_count - REACH)
    persisting_entries = jnp.where(neighbour_markers, SIBLING_COUNT, persisting_entries)
    living_markers = persisting_order_matrix < persisting_entries[:, None]
    overflow_amount = persisting_order_matrix - HOMEBOUND_LIMIT
    column_index = overflow_amount % (2 * REACH)
    sequence_extent = overflow_amount // (2 * REACH)
    step_of = jnp.where(column_index < REACH, column_index - REACH, column_index - REACH + 1)
    resident_processor = device_ids[:, None]
    remaining_here = persisting_order_matrix < HOMEBOUND_LIMIT
    target_dev = jnp.where(remaining_here, resident_processor, (resident_processor + step_of) % processor_count)
    destination_place = jnp.where(remaining_here, persisting_order_matrix, HOMEBOUND_LIMIT + TRANSFER_LIMIT * column_index + sequence_extent)
    new_slot = jnp.where(living_markers, target_dev * SIBLING_COUNT + destination_place, -1)
    return (living_markers.astype(jnp.int32).reshape(-1), new_slot.astype(jnp.int32).reshape(-1))


def prompt_table(key):
    processor_count = CONT // SIBLING_COUNT
    random_seeds = jax.random.split(jax.random.fold_in(key, 202), processor_count)
    persisting_order_matrix = jax.vmap(lambda solitary_entry: jax.random.permutation(solitary_entry, SIBLING_COUNT))(random_seeds)
    resident_processor = jnp.arange(processor_count, dtype=jnp.int32)[:, None]
    question_text = jnp.where(persisting_order_matrix < SIBLING_COUNT // 2, resident_processor, (resident_processor - 1) % processor_count)
    return question_text.astype(jnp.int32).reshape(-1)


def draw_survived(key, part):
    return route_tables(key)[0]


def draw_new_slot(key, part):
    return route_tables(key)[1]


def draw_prompt_of(key, part):
    return prompt_table(key)


def draw_prompt_rope(key, part):
    values = jnp.clip(jax.random.normal(jax.random.fold_in(key, 304), (PROMPTS, DR, PLEN), jnp.float32), -6.0, 6.0)
    return values.astype(jnp.bfloat16)


def draw_queries(key, part):
    values = 1.2 * jnp.clip(jax.random.normal(jax.random.fold_in(key, 306), (CONT, STEPS, NH, DC + DR), jnp.float32), -6.0, 6.0)
    return values.astype(jnp.bfloat16)


def draw_new_keys(key, part):
    values = jnp.clip(jax.random.normal(jax.random.fold_in(key, 309), (CONT, STEPS, DC + DR), jnp.float32), -6.0, 6.0)
    return values.astype(jnp.bfloat16)


def with_ends(values, rng, least, high):
    longest = values.shape.index(max(values.shape))
    spots = []
    for shift in (0, 1):
        where = [jax.random.randint(jax.random.fold_in(rng, axis), (), 0, length) for axis, length in enumerate(values.shape)]
        where[longest] = (where[longest] + shift) % values.shape[longest]
        spots.append(tuple(where))
    return values.at[spots[0]].set(least).at[spots[1]].set(high)


def block_levels(key, extent, cuts, smallest, top_value):
    def one(axis_at, blocks):
        steps = jax.random.uniform(jax.random.fold_in(jax.random.fold_in(key, 6), axis_at), (blocks,), jnp.float32, smallest / len(cuts), top_value / len(cuts))
        return jnp.repeat(jnp.exp(steps), extent[axis_at] // blocks).reshape((-1,) + (1,) * (len(extent) - axis_at - 1))

    level = one(*cuts[0])
    for cut in cuts[1:]:
        level = level * one(*cut)
    return level


def scatter_about(rng, shape, scale, reach, cuts=(), kind=jnp.bfloat16):
    loudness = block_levels(rng, shape, cuts, -0.22, 0.18) if cuts else 1.0
    values = jax.random.normal(rng, shape, jnp.float32) * scale * loudness
    return jnp.minimum(jnp.maximum(values, -reach), reach).astype(kind)


def setup_inputs(seed: int = 0, part: int = 0) -> dict:
    keys = jax.random.split(jax.random.key(seed), 11)
    part_splits = jax.random.split(jax.random.fold_in(keys[10], part), 11)
    return {
        "prompt_latent": scatter_about(part_splits[0], (PROMPTS, PLEN, DC), 1.0, 6.0, ((0, 16),)),
        "prompt_rope": draw_prompt_rope(jax.random.fold_in(jax.random.fold_in(keys[10], part), 71), part),
        "private_latent": scatter_about(part_splits[2], (CONT, BLK, DC), 1.0, 6.0, ((0, 16),)),
        "private_rope": scatter_about(part_splits[3], (CONT, DR, BLK), 1.0, 6.0, ((0, 16),)),
        "lengths": with_ends(jax.random.randint(part_splits[4], (CONT,), 1, BLK + 1), jax.random.fold_in(part_splits[4], 1), 1, BLK).astype(jnp.int32),
        "survived": draw_survived(jax.random.fold_in(jax.random.fold_in(keys[10], part), 71), part),
        "prompt_of": draw_prompt_of(jax.random.fold_in(jax.random.fold_in(keys[10], part), 71), part),
        "new_slot": draw_new_slot(jax.random.fold_in(jax.random.fold_in(keys[10], part), 71), part),
        "queries": draw_queries(jax.random.fold_in(jax.random.fold_in(keys[10], part), 71), part),
        "new_keys": draw_new_keys(jax.random.fold_in(jax.random.fold_in(keys[10], part), 71), part),
    }


def attend(queries, new_keys, prompt_latent, prompt_rope, private_latent, private_rope, length):
    step_count, head_count, full_width = queries.shape
    lat_width = prompt_latent.shape[1]
    prompt_len = prompt_latent.shape[0]
    block_len = private_latent.shape[0]
    query_rows = queries.reshape(step_count * head_count, full_width)
    latent = jnp.concatenate([prompt_latent, private_latent, new_keys[:, :lat_width]], axis=0)
    rope_keys = jnp.concatenate([prompt_rope, private_rope, new_keys[:, lat_width:].T], axis=1)
    scores = lax.dot_general(query_rows[:, :lat_width], latent, (((1,), (1,)), ((), ())), preferred_element_type=jnp.float32)
    scores = scores + jnp.dot(query_rows[:, lat_width:], rope_keys, preferred_element_type=jnp.float32)
    scores = scores * ((NOPE + DR) ** -0.5)
    position = jnp.arange(latent.shape[0], dtype=jnp.int32)
    inner_pos = position - prompt_len
    usable = (position < prompt_len) | ((inner_pos >= 0) & (inner_pos < length))
    newest = position - prompt_len - block_len
    step_of_row = jnp.arange(step_count * head_count, dtype=jnp.int32) // head_count
    visible = usable[None, :] | ((newest[None, :] >= 0) & (newest[None, :] <= step_of_row[:, None]))
    scores = jnp.where(visible, scores, -1e30)
    row_top = jnp.max(scores, axis=1, keepdims=True)
    weights = jnp.exp(scores - row_top)
    totals = jnp.sum(weights, axis=1, keepdims=True)
    mixed = jnp.dot(weights.astype(jnp.bfloat16), latent, preferred_element_type=jnp.float32) / totals
    return mixed.astype(jnp.bfloat16).reshape(step_count, head_count, lat_width)


def reference(prompt_latent, prompt_rope, private_latent, private_rope, lengths, survived, prompt_of, new_slot, queries, new_keys):
    slot_total = queries.shape[0]
    cont_total = lengths.shape[0]
    cont_ids = jnp.arange(cont_total, dtype=jnp.int32)
    target = jnp.where(survived > 0, new_slot, slot_total).astype(jnp.int32)
    source = jnp.full((slot_total,), -1, jnp.int32).at[target].set(cont_ids, mode="drop")

    def per_slot(slot_id):
        cont_id = source[slot_id]
        is_live = cont_id >= 0
        cont_id = jnp.maximum(cont_id, 0)
        question_text = prompt_of[cont_id]
        result = attend(queries[slot_id], new_keys[slot_id], prompt_latent[question_text], prompt_rope[question_text], private_latent[cont_id], private_rope[cont_id], lengths[cont_id])
        return jnp.where(is_live, result, jnp.zeros_like(result))

    return lax.map(per_slot, jnp.arange(slot_total, dtype=jnp.int32))
```

```python
import functools
import math

import jax
import jax.numpy as jnp
from jax import lax
from jax.experimental import pallas as pl
from jax.experimental.pallas import tpu as pltpu
from jax.sharding import PartitionSpec as P

DR = 64
NOPE = 128
REACH = 2
TRANSFER_LIMIT = 2
FRESH_ROWS = 16
CHUNKS = 4
MESH = pl.DeviceIdType.MESH
OFFSETS = tuple(o for o in range(-REACH, REACH + 1) if o != 0)
NT = (((1,), (1,)), ((), ()))


def scores_of(q, latent, rope):
    width = latent.shape[1]
    s = lax.dot_general(q[:, :width], latent, NT, preferred_element_type=jnp.float32)
    return s + jnp.dot(q[:, width:], rope, preferred_element_type=jnp.float32)


def kernel(
    n, heads,
    slot_s, prompt_s, length_s, slot_v, q_hbm, nk_hbm, lat_hbm, rope_hbm, plat_hbm, prope_hbm,
    out_hbm,
    qin, qsend, qrecv, qg, nkg, lat, rope, prior_lat, prior_rope, plat, prope,
    m_ref, l_ref, acc_ref, res, osend, orecv, out_v,
    meta_v, meta_s, rank_s, order_s, qidx_s, src_s, osel_s,
    in_sem, meta_send, meta_recv, meta_local, q_send, q_recv, p_send, p_recv, o_send, o_recv, out_sem,
):
    me = lax.axis_index("seq")
    members, rows, width = qin.shape[0], res.shape[1], lat.shape[1]
    group = members // 2
    plen = lat.shape[0]
    chunk = plen // CHUNKS
    coef = (NOPE + DR) ** (-0.5) * math.log2(math.e)
    lo = me * members
    peers = [lax.rem(me + o + n, n) for o in OFFSETS]
    nxt = lax.rem(me + 1, n)
    last = len(OFFSETS) - 1

    local = [
        pltpu.make_async_copy(q_hbm, qin.at[:, pl.ds(0, rows), :], in_sem.at[0]),
        pltpu.make_async_copy(nk_hbm, qin.at[:, pl.ds(rows, FRESH_ROWS), :], in_sem.at[1]),
        pltpu.make_async_copy(plat_hbm, plat, in_sem.at[2]),
        pltpu.make_async_copy(prope_hbm, prope, in_sem.at[3]),
        pltpu.make_async_copy(lat_hbm, lat, in_sem.at[4]),
        pltpu.make_async_copy(rope_hbm, rope, in_sem.at[5]),
    ]
    for c in local:
        c.start()

    barrier = pltpu.get_barrier_semaphore()
    for peer in peers:
        pl.semaphore_signal(barrier, inc=1, device_id={"seq": peer}, device_id_type=MESH)
    pl.semaphore_wait(barrier, len(OFFSETS))

    meta = []
    for k in range(len(OFFSETS)):
        meta.append(pltpu.make_async_remote_copy(
            src_ref=slot_v, dst_ref=meta_v.at[k], send_sem=meta_send.at[k], recv_sem=meta_recv.at[k],
            device_id={"seq": peers[k]}, device_id_type=MESH))
        meta[k].start()

    prompt_copies = []
    for j in range(CHUNKS):
        part = pl.ds(j * chunk, chunk)
        prompt_copies.append((
            pltpu.make_async_remote_copy(
                src_ref=lat_hbm.at[part, :], dst_ref=prior_lat.at[part, :],
                send_sem=p_send.at[2 * j], recv_sem=p_recv.at[2 * j],
                device_id={"seq": nxt}, device_id_type=MESH),
            pltpu.make_async_remote_copy(
                src_ref=rope_hbm.at[:, part], dst_ref=prior_rope.at[:, part],
                send_sem=p_send.at[2 * j + 1], recv_sem=p_recv.at[2 * j + 1],
                device_id={"seq": nxt}, device_id_type=MESH),
        ))
    for c in prompt_copies[0]:
        c.start()

    zero = jnp.int32(0)

    def route(c, carry):
        own_count, prior_count, counts, sel = carry
        ns = slot_s[c]
        is_own = jnp.where(prompt_s[c] == me, 1, 0)
        rank = jnp.where(is_own == 1, own_count, group + prior_count)
        rank = jnp.minimum(rank, members - 1)
        rank_s[c] = rank
        place = jnp.where((ns >= lo) & (ns < lo + members), ns - lo, 0)
        counts, sel = list(counts), list(sel)
        for k in range(len(OFFSETS)):
            base = peers[k] * members
            hit = (ns >= base) & (ns < base + members)
            for r in range(TRANSFER_LIMIT):
                this = hit & (counts[k] == r)
                sel[k * TRANSFER_LIMIT + r] = jnp.where(this, rank, sel[k * TRANSFER_LIMIT + r])
                place = jnp.where(this, members + k * TRANSFER_LIMIT + r, place)
            counts[k] = counts[k] + jnp.where(hit, 1, 0)
        qidx_s[c] = place
        return own_count + is_own, prior_count + 1 - is_own, tuple(counts), tuple(sel)

    slots = len(OFFSETS) * TRANSFER_LIMIT
    routed = lax.fori_loop(
        0, members, route, (zero, zero, (zero,) * len(OFFSETS), (zero,) * slots))
    for i in range(slots):
        osel_s[i] = routed[3][i]

    def invert(p, _):
        order_s[p] = lax.fori_loop(
            0, members, lambda c, at: jnp.where(rank_s[c] == p, c, at), zero)
        return 0

    lax.fori_loop(0, members, invert, 0)

    for k in range(len(OFFSETS)):
        meta[k].wait_recv()
    to_smem = pltpu.make_async_copy(meta_v, meta_s, meta_local)
    to_smem.start()
    local[0].wait()
    local[1].wait()
    to_smem.wait()

    def claims(k):
        def step(c, carry):
            count, found = carry
            ns = meta_s[k, 0, c]
            hit = (ns >= lo) & (ns < lo + members)
            found = tuple(
                jnp.where(hit & (count == r), ns - lo, found[r]) for r in range(TRANSFER_LIMIT))
            return count + jnp.where(hit, 1, 0), found
        return lax.fori_loop(0, members, step, (zero, (zero - 1,) * TRANSFER_LIMIT))[1]

    claimed = []
    q_copies = []
    for k in range(len(OFFSETS)):
        found = claims(k)
        claimed.extend(found)
        for r in range(TRANSFER_LIMIT):
            qsend[k, r] = qin[jnp.maximum(found[r], 0)]
        span = pl.ds(k * TRANSFER_LIMIT, TRANSFER_LIMIT)
        q_copies.append(pltpu.make_async_remote_copy(
            src_ref=qsend.at[k], dst_ref=qrecv.at[span], send_sem=q_send.at[k], recv_sem=q_recv.at[k],
            device_id={"seq": peers[last - k]}, device_id_type=MESH))
        q_copies[k].start()
    for j in range(1, CHUNKS):
        for c in prompt_copies[j]:
            c.start()

    def sources(s, _):
        at = lax.fori_loop(
            0, members, lambda c, v: jnp.where(slot_s[c] == lo + s, rank_s[c], v), zero + members)
        for i in range(slots):
            at = jnp.where(claimed[i] == s, members + 1 + i, at)
        src_s[s] = at
        return 0

    lax.fori_loop(0, members, sources, 0)
    res[members] = jnp.zeros(res.shape[1:], res.dtype)

    for c in local[2:]:
        c.wait()
    for k in range(len(OFFSETS)):
        q_copies[k].wait_recv()

    lane = lax.broadcasted_iota(jnp.int32, (rows, plat.shape[1]), 1)
    fresh_col = lax.broadcasted_iota(jnp.int32, (rows, FRESH_ROWS), 1)
    fresh_row = lax.broadcasted_iota(jnp.int32, (rows, FRESH_ROWS), 0)
    fresh_ok = fresh_col * heads <= fresh_row
    first_lane = lane == 0

    def begin(p, _):
        c = order_s[p]
        at = qidx_s[c]
        moved = at >= members
        ext = jnp.where(moved, qrecv[jnp.maximum(at - members, 0)], qin[jnp.minimum(at, members - 1)])
        q = ext[:rows]
        nk = ext[rows:]
        span = pl.ds(pl.multiple_of(p * rows, rows), rows)
        qg[span, :] = q
        block = plat[c]
        s1 = jnp.where(lane < length_s[c], scores_of(q, block, prope[c]), -1e30)
        s2 = lax.dot_general(q, nk, NT, preferred_element_type=jnp.float32)
        s2 = jnp.where(fresh_ok, s2, -1e30)
        top = jnp.maximum(jnp.max(s1, axis=1, keepdims=True), jnp.max(s2, axis=1, keepdims=True))
        w1 = jnp.exp2((s1 - top) * coef)
        w2 = jnp.exp2((s2 - top) * coef)
        m_ref[span, :] = jnp.broadcast_to(top, (rows, m_ref.shape[1]))
        l_ref[span, :] = w1 + jnp.where(first_lane, jnp.sum(w2, axis=1, keepdims=True), 0.0)
        acc_ref[span, :] = jnp.dot(
            w1.astype(jnp.bfloat16), block, preferred_element_type=jnp.float32
        ) + jnp.dot(w2.astype(jnp.bfloat16), nk[:, :width], preferred_element_type=jnp.float32)
        return 0

    lax.fori_loop(0, members, begin, 0)

    rb = 2 * rows
    lanes = m_ref.shape[1]

    def shared(lat_ref, rope_ref, j, first):
        part = pl.ds(j * chunk, chunk)

        def step(b, _):
            span = pl.ds(pl.multiple_of(first + b * rb, rb), rb)
            s = scores_of(qg[span, :], lat_ref[part, :], rope_ref[:, part])
            before = m_ref[span, :]
            top = jnp.maximum(before, jnp.max(s, axis=1, keepdims=True))
            fade = jnp.exp2((before - top) * coef)
            pieces = [
                jnp.exp2((s[:, i * lanes:(i + 1) * lanes] - top) * coef)
                for i in range(chunk // lanes)
            ]
            m_ref[span, :] = top
            l_ref[span, :] = l_ref[span, :] * fade + functools.reduce(jnp.add, pieces)
            w = jnp.concatenate([x.astype(jnp.bfloat16) for x in pieces], axis=1)
            mix = jnp.dot(w, lat_ref[part, :], preferred_element_type=jnp.float32)
            acc_ref[span, :] = (
                acc_ref[span, :] * jnp.concatenate([fade] * (width // lanes), axis=1) + mix)
            return 0

        lax.fori_loop(0, group * rows // rb, step, 0)

    def finish(p, _):
        span = pl.ds(pl.multiple_of(p * rows, rows), rows)
        total = jnp.sum(l_ref[span, :], axis=1, keepdims=True)
        res[p] = (acc_ref[span, :] / total).astype(res.dtype)
        return 0

    for j in range(CHUNKS):
        shared(lat, rope, j, 0)
    lax.fori_loop(0, group, finish, 0)
    for j in range(CHUNKS):
        for c in prompt_copies[j]:
            c.wait_recv()
        shared(prior_lat, prior_rope, j, group * rows)
    lax.fori_loop(group, members, finish, 0)

    o_copies = []
    for k in range(len(OFFSETS)):
        for r in range(TRANSFER_LIMIT):
            osend[k, r] = res[osel_s[k * TRANSFER_LIMIT + r]]
        span = pl.ds(k * TRANSFER_LIMIT, TRANSFER_LIMIT)
        o_copies.append(pltpu.make_async_remote_copy(
            src_ref=osend.at[k], dst_ref=orecv.at[span], send_sem=o_send.at[k], recv_sem=o_recv.at[k],
            device_id={"seq": peers[k]}, device_id_type=MESH))
        o_copies[k].start()
    for k in range(len(OFFSETS)):
        o_copies[k].wait_recv()

    def place(s, _):
        at = src_s[s]
        out_v[s] = jnp.where(
            at > members, orecv[jnp.maximum(at - members - 1, 0)], res[jnp.minimum(at, members)])
        return 0

    half = members // 2
    writes = []
    for h in range(2):
        lax.fori_loop(h * half, (h + 1) * half, place, 0)
        writes.append(pltpu.make_async_copy(
            out_v.at[pl.ds(h * half, half)], out_hbm.at[pl.ds(h * half, half)], out_sem.at[h]))
        writes[h].start()
    for w in writes:
        w.wait()
    for c in meta + q_copies + o_copies:
        c.wait_send()
    for pair in prompt_copies:
        for c in pair:
            c.wait_send()


def per_device(
    prompt_latent, prompt_rope, private_latent, private_rope,
    lengths, survived, prompt_of, new_slot, queries, new_keys,
):
    n = lax.axis_size("seq")
    members, steps, heads, full = queries.shape
    rows = steps * heads
    width = prompt_latent.shape[2]
    plen = prompt_latent.shape[1]
    block = private_latent.shape[1]
    rot = full - width
    kinds = len(OFFSETS)
    slots = kinds * TRANSFER_LIMIT
    fresh = jnp.pad(new_keys, ((0, 0), (0, FRESH_ROWS - steps), (0, 0)))
    bf, f32, i32 = jnp.bfloat16, jnp.float32, jnp.int32
    ext = rows + FRESH_ROWS
    smem = pl.BlockSpec(memory_space=pltpu.SMEM)
    hbm = pl.BlockSpec(memory_space=pl.ANY)
    dma = pltpu.SemaphoreType.DMA
    out = pl.pallas_call(
        functools.partial(kernel, n, heads),
        out_shape=jax.ShapeDtypeStruct((members, rows, width), bf),
        in_specs=[smem, smem, smem, pl.BlockSpec(memory_space=pltpu.VMEM)] + [hbm] * 6,
        out_specs=hbm,
        scratch_shapes=[
            pltpu.VMEM((members, ext, full), bf),
            pltpu.VMEM((kinds, TRANSFER_LIMIT, ext, full), bf),
            pltpu.VMEM((slots, ext, full), bf),
            pltpu.VMEM((members * rows, full), bf),
            pltpu.VMEM((FRESH_ROWS, full), bf),
            pltpu.VMEM((plen, width), bf),
            pltpu.VMEM((rot, plen), bf),
            pltpu.VMEM((plen, width), bf),
            pltpu.VMEM((rot, plen), bf),
            pltpu.VMEM((members, block, width), bf),
            pltpu.VMEM((members, rot, block), bf),
            pltpu.VMEM((members * rows, block), f32),
            pltpu.VMEM((members * rows, block), f32),
            pltpu.VMEM((members * rows, width), f32),
            pltpu.VMEM((members + 1, rows, width), bf),
            pltpu.VMEM((kinds, TRANSFER_LIMIT, rows, width), bf),
            pltpu.VMEM((slots, rows, width), bf),
            pltpu.VMEM((members, rows, width), bf),
            pltpu.VMEM((kinds, 1, members), i32),
            pltpu.SMEM((kinds, 1, members), i32),
            pltpu.SMEM((members,), i32),
            pltpu.SMEM((members,), i32),
            pltpu.SMEM((members,), i32),
            pltpu.SMEM((members,), i32),
            pltpu.SMEM((slots,), i32),
            dma((6,)),
            dma((kinds,)),
            dma((kinds,)),
            dma(()),
            dma((kinds,)),
            dma((kinds,)),
            dma((2 * CHUNKS,)),
            dma((2 * CHUNKS,)),
            dma((kinds,)),
            dma((kinds,)),
            dma((2,)),
        ],
        compiler_params=pltpu.CompilerParams(
            collective_id=0, has_side_effects=True, vmem_limit_bytes=56 * 2**20),
    )(
        new_slot, prompt_of, lengths, new_slot.reshape(1, members),
        queries.reshape(members, rows, full), fresh,
        prompt_latent[0], prompt_rope[0], private_latent, private_rope,
    )
    return out.reshape(members, steps, heads, width)


def solution(mesh):
    lead = ("rep", "seq")
    return jax.shard_map(
        per_device,
        mesh=mesh,
        in_specs=(
            P(lead, None, None), P(lead, None, None), P(lead, None, None), P(lead, None, None),
            P(lead), P(lead), P(lead), P(lead),
            P(lead, None, None, None), P(lead, None, None),
        ),
        out_specs=P(lead, None, None, None),
        check_vma=False,
    )
```

```python
import functools
import math

import jax
import jax.numpy as jnp
from jax import lax
from jax.experimental import pallas as pl
from jax.experimental.pallas import tpu as pltpu
from jax.sharding import PartitionSpec as P

DR = 64
NOPE = 128
REACH = 2
TRANSFER_LIMIT = 2
FRESH_ROWS = 16
CHUNKS = 4
MESH = pl.DeviceIdType.MESH
OFFSETS = tuple(o for o in range(-REACH, REACH + 1) if o != 0)
NT = (((1,), (1,)), ((), ()))


def scores_of(q_lat, q_rot, latent, rope):
    s = lax.dot_general(q_lat, latent, NT, preferred_element_type=jnp.float32)
    return s + jnp.dot(q_rot, rope, preferred_element_type=jnp.float32)


def kernel(
    n, heads,
    slot_s, prompt_s, length_s, slot_v, q_hbm, nk_hbm, lat_hbm, rope_hbm, plat_hbm, prope_hbm,
    all_hbm, src_s,
    qin, nkin, lsend, rsend, ksend, lrecv, rrecv, krecv, qg_lat, qg_rot,
    lat, rope, prior_lat, prior_rope, plat, prope,
    m_ref, l_ref, acc_ref, res, osend,
    meta_v, meta_s, rank_s, order_s, qidx_s, osel_s,
    in_sem, meta_send, meta_recv, meta_local, q_send, q_recv, p_send, p_recv, o_send, o_recv, out_sem,
):
    me = lax.axis_index("seq")
    members, rows, width = qin.shape[0], res.shape[1], lat.shape[1]
    rot = rope.shape[0]
    steps = rows // heads
    group = members // 2
    plen = lat.shape[0]
    chunk = plen // CHUNKS
    coef = (NOPE + DR) ** (-0.5) * math.log2(math.e)
    lo = me * members
    peers = [lax.rem(me + o + n, n) for o in OFFSETS]
    nxt = lax.rem(me + 1, n)
    last = len(OFFSETS) - 1

    local = [
        pltpu.make_async_copy(q_hbm, qin, in_sem.at[0]),
        pltpu.make_async_copy(nk_hbm, nkin, in_sem.at[1]),
        pltpu.make_async_copy(plat_hbm, plat, in_sem.at[2]),
        pltpu.make_async_copy(prope_hbm, prope, in_sem.at[3]),
        pltpu.make_async_copy(lat_hbm, lat, in_sem.at[4]),
        pltpu.make_async_copy(rope_hbm, rope, in_sem.at[5]),
    ]
    for c in local:
        c.start()

    barrier = pltpu.get_barrier_semaphore()
    for peer in peers:
        pl.semaphore_signal(barrier, inc=1, device_id={"seq": peer}, device_id_type=MESH)
    pl.semaphore_wait(barrier, len(OFFSETS))

    meta = []
    for k in range(len(OFFSETS)):
        meta.append(pltpu.make_async_remote_copy(
            src_ref=slot_v, dst_ref=meta_v.at[k], send_sem=meta_send.at[k], recv_sem=meta_recv.at[k],
            device_id={"seq": peers[k]}, device_id_type=MESH))
        meta[k].start()

    prompt_copies = []
    for j in range(CHUNKS):
        part = pl.ds(j * chunk, chunk)
        prompt_copies.append((
            pltpu.make_async_remote_copy(
                src_ref=lat_hbm.at[part, :], dst_ref=prior_lat.at[part, :],
                send_sem=p_send.at[2 * j], recv_sem=p_recv.at[2 * j],
                device_id={"seq": nxt}, device_id_type=MESH),
            pltpu.make_async_remote_copy(
                src_ref=rope_hbm.at[:, part], dst_ref=prior_rope.at[:, part],
                send_sem=p_send.at[2 * j + 1], recv_sem=p_recv.at[2 * j + 1],
                device_id={"seq": nxt}, device_id_type=MESH),
        ))
    for c in prompt_copies[0]:
        c.start()

    zero = jnp.int32(0)

    def route(c, carry):
        own_count, prior_count, counts, sel = carry
        ns = slot_s[c]
        is_own = jnp.where(prompt_s[c] == me, 1, 0)
        rank = jnp.where(is_own == 1, own_count, group + prior_count)
        rank = jnp.minimum(rank, members - 1)
        rank_s[c] = rank
        place = jnp.where((ns >= lo) & (ns < lo + members), ns - lo, 0)
        counts, sel = list(counts), list(sel)
        for k in range(len(OFFSETS)):
            base = peers[k] * members
            hit = (ns >= base) & (ns < base + members)
            for r in range(TRANSFER_LIMIT):
                this = hit & (counts[k] == r)
                sel[k * TRANSFER_LIMIT + r] = jnp.where(this, rank, sel[k * TRANSFER_LIMIT + r])
                place = jnp.where(this, members + k * TRANSFER_LIMIT + r, place)
            counts[k] = counts[k] + jnp.where(hit, 1, 0)
        qidx_s[c] = place
        return own_count + is_own, prior_count + 1 - is_own, tuple(counts), tuple(sel)

    slots = len(OFFSETS) * TRANSFER_LIMIT
    routed = lax.fori_loop(
        0, members, route, (zero, zero, (zero,) * len(OFFSETS), (zero,) * slots))
    for i in range(slots):
        osel_s[i] = routed[3][i]

    def invert(p, _):
        order_s[p] = lax.fori_loop(
            0, members, lambda c, at: jnp.where(rank_s[c] == p, c, at), zero)
        return 0

    lax.fori_loop(0, members, invert, 0)

    for k in range(len(OFFSETS)):
        meta[k].wait_recv()
    to_smem = pltpu.make_async_copy(meta_v, meta_s, meta_local)
    to_smem.start()
    local[0].wait()
    local[1].wait()
    to_smem.wait()

    def claims(k):
        def step(c, carry):
            count, found = carry
            ns = meta_s[k, 0, c]
            hit = (ns >= lo) & (ns < lo + members)
            found = tuple(
                jnp.where(hit & (count == r), ns - lo, found[r]) for r in range(TRANSFER_LIMIT))
            return count + jnp.where(hit, 1, 0), found
        return lax.fori_loop(0, members, step, (zero, (zero - 1,) * TRANSFER_LIMIT))[1]

    claimed = []
    q_copies = []
    for k in range(len(OFFSETS)):
        found = claims(k)
        claimed.extend(found)
        spots = [jnp.maximum(f, 0) for f in found]
        for r in range(TRANSFER_LIMIT):
            lsend[k, r] = qin[spots[r]][:, :width]
        rsend[k] = jnp.concatenate([qin[at][:, width:] for at in spots], axis=1)
        ksend[k] = functools.reduce(jnp.add, [nkin[at, r] for r, at in enumerate(spots)])
        group_copies = [
            pltpu.make_async_remote_copy(
                src_ref=src.at[k], dst_ref=dst.at[k], send_sem=q_send.at[3 * k + i],
                recv_sem=q_recv.at[3 * k + i],
                device_id={"seq": peers[last - k]}, device_id_type=MESH)
            for i, (src, dst) in enumerate(((lsend, lrecv), (rsend, rrecv), (ksend, krecv)))
        ]
        for c in group_copies:
            c.start()
        q_copies.extend(group_copies)
    for j in range(1, CHUNKS):
        for c in prompt_copies[j]:
            c.start()

    def sources(s, _):
        at = lax.fori_loop(
            0, members, lambda c, v: jnp.where(slot_s[c] == lo + s, rank_s[c], v), zero + members)
        for i in range(slots):
            at = jnp.where(claimed[i] == s, members + 1 + i, at)
        src_s[s] = at
        return 0

    lax.fori_loop(0, members, sources, 0)
    res[members] = jnp.zeros(res.shape[1:], res.dtype)

    for c in local[2:]:
        c.wait()
    for c in q_copies:
        c.wait_recv()

    lane = lax.broadcasted_iota(jnp.int32, (rows, plat.shape[1]), 1)
    fresh_col = lax.broadcasted_iota(jnp.int32, (rows, FRESH_ROWS), 1)
    fresh_row = lax.broadcasted_iota(jnp.int32, (rows, FRESH_ROWS), 0)
    first_lane = lane == 0
    share = FRESH_ROWS // TRANSFER_LIMIT

    def begin_one(p):
        c = order_s[p]
        at = qidx_s[c]
        moved = at >= members
        far = jnp.maximum(at - members, 0)
        lane_k, turn = far // TRANSFER_LIMIT, far % TRANSFER_LIMIT
        near = jnp.minimum(at, members - 1)
        home = qin[near]
        q_lat = jnp.where(moved, lrecv[lane_k, turn], home[:, :width])
        packed = rrecv[lane_k]
        far_rot = packed[:, :rot]
        for r in range(1, TRANSFER_LIMIT):
            far_rot = jnp.where(turn == r, packed[:, r * rot:(r + 1) * rot], far_rot)
        q_rot = jnp.where(moved, far_rot, home[:, width:])
        nk = jnp.where(moved, krecv[lane_k], nkin[near, 0])
        base = jnp.where(moved, turn * share, 0)
        block = plat[c]
        s1 = jnp.where(lane < length_s[c], scores_of(q_lat, q_rot, block, prope[c]), -1e30)
        s2 = lax.dot_general(q_lat, nk[:, :width], NT, preferred_element_type=jnp.float32)
        s2 = s2 + lax.dot_general(q_rot, nk[:, width:], NT, preferred_element_type=jnp.float32)
        new = fresh_col - base
        s2 = jnp.where((new >= 0) & (new < steps) & (new * heads <= fresh_row), s2, -1e30)
        top = jnp.maximum(jnp.max(s1, axis=1, keepdims=True), jnp.max(s2, axis=1, keepdims=True))
        w1 = jnp.exp2((s1 - top) * coef)
        w2 = jnp.exp2((s2 - top) * coef)
        total = w1 + jnp.where(first_lane, jnp.sum(w2, axis=1, keepdims=True), 0.0)
        mix = jnp.dot(
            w1.astype(jnp.bfloat16), block, preferred_element_type=jnp.float32
        ) + jnp.dot(w2.astype(jnp.bfloat16), nk[:, :width], preferred_element_type=jnp.float32)
        return q_lat, q_rot, jnp.broadcast_to(top, (rows, m_ref.shape[1])), total, mix

    def begin(b, _):
        made = [begin_one(2 * b + u) for u in range(2)]
        for u in range(2):
            span = pl.ds(pl.multiple_of((2 * b + u) * rows, rows), rows)
            for ref, value in zip((qg_lat, qg_rot, m_ref, l_ref, acc_ref), made[u]):
                ref[span, :] = value
        return 0

    lax.fori_loop(0, members // 2, begin, 0)

    rb = 2 * rows
    lanes = m_ref.shape[1]

    def shared(lat_ref, rope_ref, js, first, final):
        parts = [pl.ds(j * chunk, chunk) for j in js]

        def step(b, _):
            span = pl.ds(pl.multiple_of((first + 2 * b) * rows, rb), rb)
            q_lat, q_rot, before = qg_lat[span, :], qg_rot[span, :], m_ref[span, :]
            tiles = []
            for part in parts:
                s = scores_of(q_lat, q_rot, lat_ref[part, :], rope_ref[:, part])
                tiles.append([s[:, i * lanes:(i + 1) * lanes] for i in range(chunk // lanes)])
            peak = functools.reduce(jnp.maximum, [t for group_ in tiles for t in group_])
            top = jnp.maximum(before, jnp.max(peak, axis=1, keepdims=True))
            fade = jnp.exp2((before - top) * coef)
            total = l_ref[span, :] * fade
            mix = acc_ref[span, :] * jnp.concatenate([fade] * (width // lanes), axis=1)
            for part, group_ in zip(parts, tiles):
                pieces = [jnp.exp2((t - top) * coef) for t in group_]
                total = total + functools.reduce(jnp.add, pieces)
                w = jnp.concatenate([x.astype(jnp.bfloat16) for x in pieces], axis=1)
                mix = mix + jnp.dot(w, lat_ref[part, :], preferred_element_type=jnp.float32)
            if final:
                out = (mix * (1.0 / jnp.sum(total, axis=1, keepdims=True))).astype(res.dtype)
                for u in range(2):
                    res[first + 2 * b + u] = out[u * rows:(u + 1) * rows]
            else:
                m_ref[span, :] = top
                l_ref[span, :] = total
                acc_ref[span, :] = mix
            return 0

        lax.fori_loop(0, group // 2, step, 0)

    def arrive(js):
        for j in js:
            for c in prompt_copies[j]:
                c.wait_recv()

    shared(lat, rope, range(CHUNKS), 0, True)
    arrive(range(CHUNKS - 1))
    shared(prior_lat, prior_rope, range(CHUNKS - 1), group, False)
    arrive((CHUNKS - 1,))
    shared(prior_lat, prior_rope, (CHUNKS - 1,), group, True)

    o_copies = []
    for k in range(len(OFFSETS)):
        for r in range(TRANSFER_LIMIT):
            osend[k, r] = res[osel_s[k * TRANSFER_LIMIT + r]]
        span = pl.ds(members + 1 + k * TRANSFER_LIMIT, TRANSFER_LIMIT)
        o_copies.append(pltpu.make_async_remote_copy(
            src_ref=osend.at[k], dst_ref=all_hbm.at[span], send_sem=o_send.at[k], recv_sem=o_recv.at[k],
            device_id={"seq": peers[k]}, device_id_type=MESH))
        o_copies[k].start()
    keep = pltpu.make_async_copy(res, all_hbm.at[pl.ds(0, members + 1)], out_sem)
    keep.start()
    for c in meta + q_copies:
        c.wait_send()
    for pair in prompt_copies:
        for c in pair:
            c.wait_send()
    keep.wait()
    for c in o_copies:
        c.wait()


def place_kernel(src_s, all_hbm, out_hbm, sem):
    copies = [
        pltpu.make_async_copy(all_hbm.at[src_s[s]], out_hbm.at[s], sem.at[s])
        for s in range(out_hbm.shape[0])
    ]
    for c in copies:
        c.start()
    for c in copies:
        c.wait()


def per_device(
    prompt_latent, prompt_rope, private_latent, private_rope,
    lengths, survived, prompt_of, new_slot, queries, new_keys,
):
    n = lax.axis_size("seq")
    members, steps, heads, full = queries.shape
    rows = steps * heads
    width = prompt_latent.shape[2]
    plen = prompt_latent.shape[1]
    block = private_latent.shape[1]
    rot = full - width
    kinds = len(OFFSETS)
    slots = kinds * TRANSFER_LIMIT
    share = FRESH_ROWS // TRANSFER_LIMIT
    fresh = jnp.stack([
        jnp.pad(new_keys, ((0, 0), (r * share, FRESH_ROWS - steps - r * share), (0, 0)))
        for r in range(TRANSFER_LIMIT)
    ], axis=1)
    bf, f32, i32 = jnp.bfloat16, jnp.float32, jnp.int32
    smem = pl.BlockSpec(memory_space=pltpu.SMEM)
    hbm = pl.BlockSpec(memory_space=pl.ANY)
    dma = pltpu.SemaphoreType.DMA
    everything, src = pl.pallas_call(
        functools.partial(kernel, n, heads),
        out_shape=(
            jax.ShapeDtypeStruct((members + 1 + slots, rows, width), bf),
            jax.ShapeDtypeStruct((members,), i32)),
        in_specs=[smem, smem, smem, pl.BlockSpec(memory_space=pltpu.VMEM)] + [hbm] * 6,
        out_specs=(hbm, smem),
        scratch_shapes=[
            pltpu.VMEM((members, rows, full), bf),
            pltpu.VMEM((members, TRANSFER_LIMIT, FRESH_ROWS, full), bf),
            pltpu.VMEM((kinds, TRANSFER_LIMIT, rows, width), bf),
            pltpu.VMEM((kinds, rows, TRANSFER_LIMIT * rot), bf),
            pltpu.VMEM((kinds, FRESH_ROWS, full), bf),
            pltpu.VMEM((kinds, TRANSFER_LIMIT, rows, width), bf),
            pltpu.VMEM((kinds, rows, TRANSFER_LIMIT * rot), bf),
            pltpu.VMEM((kinds, FRESH_ROWS, full), bf),
            pltpu.VMEM((members * rows, width), bf),
            pltpu.VMEM((members * rows, rot), bf),
            pltpu.VMEM((plen, width), bf),
            pltpu.VMEM((rot, plen), bf),
            pltpu.VMEM((plen, width), bf),
            pltpu.VMEM((rot, plen), bf),
            pltpu.VMEM((members, block, width), bf),
            pltpu.VMEM((members, rot, block), bf),
            pltpu.VMEM((members * rows, block), f32),
            pltpu.VMEM((members * rows, block), f32),
            pltpu.VMEM((members * rows, width), f32),
            pltpu.VMEM((members + 1, rows, width), bf),
            pltpu.VMEM((kinds, TRANSFER_LIMIT, rows, width), bf),
            pltpu.VMEM((kinds, 1, members), i32),
            pltpu.SMEM((kinds, 1, members), i32),
            pltpu.SMEM((members,), i32),
            pltpu.SMEM((members,), i32),
            pltpu.SMEM((members,), i32),
            pltpu.SMEM((slots,), i32),
            dma((6,)),
            dma((kinds,)),
            dma((kinds,)),
            dma(()),
            dma((3 * kinds,)),
            dma((3 * kinds,)),
            dma((2 * CHUNKS,)),
            dma((2 * CHUNKS,)),
            dma((kinds,)),
            dma((kinds,)),
            dma(()),
        ],
        compiler_params=pltpu.CompilerParams(
            collective_id=0, has_side_effects=True, vmem_limit_bytes=56 * 2**20),
    )(
        new_slot, prompt_of, lengths, new_slot.reshape(1, members),
        queries.reshape(members, rows, full), fresh,
        prompt_latent[0], prompt_rope[0], private_latent, private_rope,
    )
    out = pl.pallas_call(
        place_kernel,
        out_shape=jax.ShapeDtypeStruct((members, rows, width), bf),
        in_specs=[smem, hbm],
        out_specs=hbm,
        scratch_shapes=[dma((members,))],
    )(src, everything)
    return out.reshape(members, steps, heads, width)


def solution(mesh):
    lead = ("rep", "seq")
    return jax.shard_map(
        per_device,
        mesh=mesh,
        in_specs=(
            P(lead, None, None), P(lead, None, None), P(lead, None, None), P(lead, None, None),
            P(lead), P(lead), P(lead), P(lead),
            P(lead, None, None, None), P(lead, None, None),
        ),
        out_specs=P(lead, None, None, None),
        check_vma=False,
    )
```

```python
import functools
import math

import jax
import jax.numpy as jnp
from jax import lax
from jax.experimental import pallas as pl
from jax.experimental.pallas import tpu as pltpu
from jax.sharding import PartitionSpec as P

DR = 64
NOPE = 128
REACH = 2
TRANSFER_LIMIT = 2
FRESH_ROWS = 16
CHUNKS = 4
MESH = pl.DeviceIdType.MESH
OFFSETS = tuple(o for o in range(-REACH, REACH + 1) if o != 0)
NT = (((1,), (1,)), ((), ()))


def scores_of(q_lat, q_rot, latent, rope):
    s = lax.dot_general(q_lat, latent, NT, preferred_element_type=jnp.float32)
    return s + jnp.dot(q_rot, rope, preferred_element_type=jnp.float32)


def kernel(
    n, heads,
    slot_s, prompt_s, length_s, slot_v, q_hbm, nk_hbm, lat_hbm, rope_hbm, plat_hbm, prope_hbm,
    all_hbm, src_s,
    qin, nkin, lsend, rsend, ksend, lrecv, rrecv, krecv, qg_lat, qg_rot,
    lat, rope, prior_lat, prior_rope, plat, prope,
    m_ref, l_ref, acc_ref, res, osend,
    meta_v, meta_s, rank_s, order_s, qidx_s, osel_s,
    in_sem, meta_send, meta_recv, meta_local, q_send, q_recv, p_send, p_recv, o_send, o_recv, out_sem,
):
    me = lax.axis_index("seq")
    members, rows, width = qin.shape[0], res.shape[1], lat.shape[1]
    rot = rope.shape[0]
    steps = rows // heads
    group = members // 2
    plen = lat.shape[0]
    chunk = plen // CHUNKS
    coef = (NOPE + DR) ** (-0.5) * math.log2(math.e)
    lo = me * members
    peers = [lax.rem(me + o + n, n) for o in OFFSETS]
    nxt = lax.rem(me + 1, n)
    last = len(OFFSETS) - 1

    local = [
        pltpu.make_async_copy(q_hbm, qin, in_sem.at[0]),
        pltpu.make_async_copy(nk_hbm, nkin, in_sem.at[1]),
        pltpu.make_async_copy(plat_hbm, plat, in_sem.at[2]),
        pltpu.make_async_copy(prope_hbm, prope, in_sem.at[3]),
        pltpu.make_async_copy(lat_hbm, lat, in_sem.at[4]),
        pltpu.make_async_copy(rope_hbm, rope, in_sem.at[5]),
    ]
    for c in local:
        c.start()

    barrier = pltpu.get_barrier_semaphore()
    for peer in peers:
        pl.semaphore_signal(barrier, inc=1, device_id={"seq": peer}, device_id_type=MESH)
    pl.semaphore_wait(barrier, len(OFFSETS))

    meta = []
    for k in range(len(OFFSETS)):
        meta.append(pltpu.make_async_remote_copy(
            src_ref=slot_v, dst_ref=meta_v.at[k], send_sem=meta_send.at[k], recv_sem=meta_recv.at[k],
            device_id={"seq": peers[k]}, device_id_type=MESH))
        meta[k].start()

    prompt_copies = []
    for j in range(CHUNKS):
        part = pl.ds(j * chunk, chunk)
        prompt_copies.append((
            pltpu.make_async_remote_copy(
                src_ref=lat_hbm.at[part, :], dst_ref=prior_lat.at[part, :],
                send_sem=p_send.at[2 * j], recv_sem=p_recv.at[2 * j],
                device_id={"seq": nxt}, device_id_type=MESH),
            pltpu.make_async_remote_copy(
                src_ref=rope_hbm.at[:, part], dst_ref=prior_rope.at[:, part],
                send_sem=p_send.at[2 * j + 1], recv_sem=p_recv.at[2 * j + 1],
                device_id={"seq": nxt}, device_id_type=MESH),
        ))
    for c in prompt_copies[0]:
        c.start()

    zero = jnp.int32(0)
    for k in range(len(OFFSETS)):
        meta[k].wait_recv()
    to_smem = pltpu.make_async_copy(meta_v, meta_s, meta_local)
    to_smem.start()
    local[0].wait()
    local[1].wait()
    to_smem.wait()

    def claims(k):
        def step(c, carry):
            count, found = carry
            ns = meta_s[k, 0, c]
            hit = (ns >= lo) & (ns < lo + members)
            found = tuple(
                jnp.where(hit & (count == r), ns - lo, found[r]) for r in range(TRANSFER_LIMIT))
            return count + jnp.where(hit, 1, 0), found
        return lax.fori_loop(0, members, step, (zero, (zero - 1,) * TRANSFER_LIMIT))[1]

    claimed = []
    q_copies = []
    for k in range(len(OFFSETS)):
        found = claims(k)
        claimed.extend(found)
        spots = [jnp.maximum(f, 0) for f in found]
        for r in range(TRANSFER_LIMIT):
            lsend[k, r] = qin[spots[r]][:, :width]
        rsend[k] = jnp.concatenate([qin[at][:, width:] for at in spots], axis=1)
        ksend[k] = functools.reduce(jnp.add, [nkin[at, r] for r, at in enumerate(spots)])
        group_copies = [
            pltpu.make_async_remote_copy(
                src_ref=src.at[k], dst_ref=dst.at[k], send_sem=q_send.at[3 * k + i],
                recv_sem=q_recv.at[3 * k + i],
                device_id={"seq": peers[last - k]}, device_id_type=MESH)
            for i, (src, dst) in enumerate(((lsend, lrecv), (rsend, rrecv), (ksend, krecv)))
        ]
        for c in group_copies:
            c.start()
        q_copies.extend(group_copies)

    def route(c, carry):
        own_count, prior_count, counts, sel = carry
        ns = slot_s[c]
        is_own = jnp.where(prompt_s[c] == me, 1, 0)
        rank = jnp.where(is_own == 1, own_count, group + prior_count)
        rank = jnp.minimum(rank, members - 1)
        rank_s[c] = rank
        place = jnp.where((ns >= lo) & (ns < lo + members), ns - lo, 0)
        counts, sel = list(counts), list(sel)
        for k in range(len(OFFSETS)):
            base = peers[k] * members
            hit = (ns >= base) & (ns < base + members)
            for r in range(TRANSFER_LIMIT):
                this = hit & (counts[k] == r)
                sel[k * TRANSFER_LIMIT + r] = jnp.where(this, rank, sel[k * TRANSFER_LIMIT + r])
                place = jnp.where(this, members + k * TRANSFER_LIMIT + r, place)
            counts[k] = counts[k] + jnp.where(hit, 1, 0)
        qidx_s[c] = place
        return own_count + is_own, prior_count + 1 - is_own, tuple(counts), tuple(sel)

    slots = len(OFFSETS) * TRANSFER_LIMIT
    routed = lax.fori_loop(
        0, members, route, (zero, zero, (zero,) * len(OFFSETS), (zero,) * slots))
    for i in range(slots):
        osel_s[i] = routed[3][i]

    def invert(p, _):
        order_s[p] = lax.fori_loop(
            0, members, lambda c, at: jnp.where(rank_s[c] == p, c, at), zero)
        return 0

    lax.fori_loop(0, members, invert, 0)

    def sources(s, _):
        at = lax.fori_loop(
            0, members, lambda c, v: jnp.where(slot_s[c] == lo + s, rank_s[c], v), zero + members)
        for i in range(slots):
            at = jnp.where(claimed[i] == s, members + 1 + i, at)
        src_s[s] = at
        return 0

    lax.fori_loop(0, members, sources, 0)
    res[members] = jnp.zeros(res.shape[1:], res.dtype)

    for c in q_copies:
        c.wait_send()
    for j in range(1, CHUNKS):
        for c in prompt_copies[j]:
            c.start()
    for c in local[2:]:
        c.wait()
    for c in q_copies:
        c.wait_recv()

    lane = lax.broadcasted_iota(jnp.int32, (rows, plat.shape[1]), 1)
    fresh_col = lax.broadcasted_iota(jnp.int32, (rows, FRESH_ROWS), 1)
    fresh_row = lax.broadcasted_iota(jnp.int32, (rows, FRESH_ROWS), 0)
    first_lane = lane == 0
    share = FRESH_ROWS // TRANSFER_LIMIT

    def begin_one(p):
        c = order_s[p]
        at = qidx_s[c]
        moved = at >= members
        far = jnp.maximum(at - members, 0)
        lane_k, turn = far // TRANSFER_LIMIT, far % TRANSFER_LIMIT
        near = jnp.minimum(at, members - 1)
        home = qin[near]
        q_lat = jnp.where(moved, lrecv[lane_k, turn], home[:, :width])
        packed = rrecv[lane_k]
        far_rot = packed[:, :rot]
        for r in range(1, TRANSFER_LIMIT):
            far_rot = jnp.where(turn == r, packed[:, r * rot:(r + 1) * rot], far_rot)
        q_rot = jnp.where(moved, far_rot, home[:, width:])
        nk = jnp.where(moved, krecv[lane_k], nkin[near, 0])
        base = jnp.where(moved, turn * share, 0)
        block = plat[c]
        s1 = jnp.where(lane < length_s[c], scores_of(q_lat, q_rot, block, prope[c]), -1e30)
        s2 = lax.dot_general(q_lat, nk[:, :width], NT, preferred_element_type=jnp.float32)
        s2 = s2 + lax.dot_general(q_rot, nk[:, width:], NT, preferred_element_type=jnp.float32)
        new = fresh_col - base
        s2 = jnp.where((new >= 0) & (new < steps) & (new * heads <= fresh_row), s2, -1e30)
        top = jnp.maximum(jnp.max(s1, axis=1, keepdims=True), jnp.max(s2, axis=1, keepdims=True))
        w1 = jnp.exp2((s1 - top) * coef)
        w2 = jnp.exp2((s2 - top) * coef)
        total = w1 + jnp.where(first_lane, jnp.sum(w2, axis=1, keepdims=True), 0.0)
        mix = jnp.dot(
            w1.astype(jnp.bfloat16), block, preferred_element_type=jnp.float32
        ) + jnp.dot(w2.astype(jnp.bfloat16), nk[:, :width], preferred_element_type=jnp.float32)
        return q_lat, q_rot, jnp.broadcast_to(top, (rows, m_ref.shape[1])), total, mix

    def begin(b, _):
        made = [begin_one(2 * b + u) for u in range(2)]
        for u in range(2):
            span = pl.ds(pl.multiple_of((2 * b + u) * rows, rows), rows)
            for ref, value in zip((qg_lat, qg_rot, m_ref, l_ref, acc_ref), made[u]):
                ref[span, :] = value
        return 0

    lax.fori_loop(0, members // 2, begin, 0)

    rb = 2 * rows
    lanes = m_ref.shape[1]

    def shared(lat_ref, rope_ref, js, first, final):
        parts = [pl.ds(j * chunk, chunk) for j in js]

        def step(b, _):
            span = pl.ds(pl.multiple_of((first + 2 * b) * rows, rb), rb)
            q_lat, q_rot, before = qg_lat[span, :], qg_rot[span, :], m_ref[span, :]
            tiles = []
            for part in parts:
                s = scores_of(q_lat, q_rot, lat_ref[part, :], rope_ref[:, part])
                tiles.append([s[:, i * lanes:(i + 1) * lanes] for i in range(chunk // lanes)])
            peak = functools.reduce(jnp.maximum, [t for group_ in tiles for t in group_])
            top = jnp.maximum(before, jnp.max(peak, axis=1, keepdims=True))
            fade = jnp.exp2((before - top) * coef)
            total = l_ref[span, :] * fade
            mix = acc_ref[span, :] * jnp.concatenate([fade] * (width // lanes), axis=1)
            for part, group_ in zip(parts, tiles):
                pieces = [jnp.exp2((t - top) * coef) for t in group_]
                total = total + functools.reduce(jnp.add, pieces)
                w = jnp.concatenate([x.astype(jnp.bfloat16) for x in pieces], axis=1)
                mix = mix + jnp.dot(w, lat_ref[part, :], preferred_element_type=jnp.float32)
            if final:
                out = (mix * (1.0 / jnp.sum(total, axis=1, keepdims=True))).astype(res.dtype)
                for u in range(2):
                    res[first + 2 * b + u] = out[u * rows:(u + 1) * rows]
            else:
                m_ref[span, :] = top
                l_ref[span, :] = total
                acc_ref[span, :] = mix
            return 0

        lax.fori_loop(0, group // 2, step, 0)

    def arrive(js):
        for j in js:
            for c in prompt_copies[j]:
                c.wait_recv()

    shared(lat, rope, range(CHUNKS), 0, True)
    arrive(range(CHUNKS - 1))
    shared(prior_lat, prior_rope, range(CHUNKS - 1), group, False)
    arrive((CHUNKS - 1,))
    shared(prior_lat, prior_rope, (CHUNKS - 1,), group, True)

    o_copies = []
    for k in range(len(OFFSETS)):
        for r in range(TRANSFER_LIMIT):
            osend[k, r] = res[osel_s[k * TRANSFER_LIMIT + r]]
        span = pl.ds(members + 1 + k * TRANSFER_LIMIT, TRANSFER_LIMIT)
        o_copies.append(pltpu.make_async_remote_copy(
            src_ref=osend.at[k], dst_ref=all_hbm.at[span], send_sem=o_send.at[k], recv_sem=o_recv.at[k],
            device_id={"seq": peers[k]}, device_id_type=MESH))
        o_copies[k].start()
    keep = pltpu.make_async_copy(res, all_hbm.at[pl.ds(0, members + 1)], out_sem)
    keep.start()
    for c in meta:
        c.wait_send()
    for pair in prompt_copies:
        for c in pair:
            c.wait_send()
    keep.wait()
    for c in o_copies:
        c.wait()


def place_kernel(src_s, all_hbm, out_hbm, block, in_sem, out_sem):
    members = out_hbm.shape[0]
    reads = [
        pltpu.make_async_copy(all_hbm.at[src_s[s]], block.at[s], in_sem.at[s]) for s in range(members)
    ]
    writes = [
        pltpu.make_async_copy(block.at[s], out_hbm.at[s], out_sem.at[s]) for s in range(members)
    ]
    for c in reads:
        c.start()
    for read, write in zip(reads, writes):
        read.wait()
        write.start()
    for c in writes:
        c.wait()


def per_device(
    prompt_latent, prompt_rope, private_latent, private_rope,
    lengths, survived, prompt_of, new_slot, queries, new_keys,
):
    n = lax.axis_size("seq")
    members, steps, heads, full = queries.shape
    rows = steps * heads
    width = prompt_latent.shape[2]
    plen = prompt_latent.shape[1]
    block = private_latent.shape[1]
    rot = full - width
    kinds = len(OFFSETS)
    slots = kinds * TRANSFER_LIMIT
    share = FRESH_ROWS // TRANSFER_LIMIT
    fresh = jnp.stack([
        jnp.pad(new_keys, ((0, 0), (r * share, FRESH_ROWS - steps - r * share), (0, 0)))
        for r in range(TRANSFER_LIMIT)
    ], axis=1)
    bf, f32, i32 = jnp.bfloat16, jnp.float32, jnp.int32
    smem = pl.BlockSpec(memory_space=pltpu.SMEM)
    hbm = pl.BlockSpec(memory_space=pl.ANY)
    dma = pltpu.SemaphoreType.DMA
    everything, src = pl.pallas_call(
        functools.partial(kernel, n, heads),
        out_shape=(
            jax.ShapeDtypeStruct((members + 1 + slots, rows, width), bf),
            jax.ShapeDtypeStruct((members,), i32)),
        in_specs=[smem, smem, smem, pl.BlockSpec(memory_space=pltpu.VMEM)] + [hbm] * 6,
        out_specs=(hbm, smem),
        scratch_shapes=[
            pltpu.VMEM((members, rows, full), bf),
            pltpu.VMEM((members, TRANSFER_LIMIT, FRESH_ROWS, full), bf),
            pltpu.VMEM((kinds, TRANSFER_LIMIT, rows, width), bf),
            pltpu.VMEM((kinds, rows, TRANSFER_LIMIT * rot), bf),
            pltpu.VMEM((kinds, FRESH_ROWS, full), bf),
            pltpu.VMEM((kinds, TRANSFER_LIMIT, rows, width), bf),
            pltpu.VMEM((kinds, rows, TRANSFER_LIMIT * rot), bf),
            pltpu.VMEM((kinds, FRESH_ROWS, full), bf),
            pltpu.VMEM((members * rows, width), bf),
            pltpu.VMEM((members * rows, rot), bf),
            pltpu.VMEM((plen, width), bf),
            pltpu.VMEM((rot, plen), bf),
            pltpu.VMEM((plen, width), bf),
            pltpu.VMEM((rot, plen), bf),
            pltpu.VMEM((members, block, width), bf),
            pltpu.VMEM((members, rot, block), bf),
            pltpu.VMEM((members * rows, block), f32),
            pltpu.VMEM((members * rows, block), f32),
            pltpu.VMEM((members * rows, width), f32),
            pltpu.VMEM((members + 1, rows, width), bf),
            pltpu.VMEM((kinds, TRANSFER_LIMIT, rows, width), bf),
            pltpu.VMEM((kinds, 1, members), i32),
            pltpu.SMEM((kinds, 1, members), i32),
            pltpu.SMEM((members,), i32),
            pltpu.SMEM((members,), i32),
            pltpu.SMEM((members,), i32),
            pltpu.SMEM((slots,), i32),
            dma((6,)),
            dma((kinds,)),
            dma((kinds,)),
            dma(()),
            dma((3 * kinds,)),
            dma((3 * kinds,)),
            dma((2 * CHUNKS,)),
            dma((2 * CHUNKS,)),
            dma((kinds,)),
            dma((kinds,)),
            dma(()),
        ],
        compiler_params=pltpu.CompilerParams(
            collective_id=0, has_side_effects=True, vmem_limit_bytes=56 * 2**20),
    )(
        new_slot, prompt_of, lengths, new_slot.reshape(1, members),
        queries.reshape(members, rows, full), fresh,
        prompt_latent[0], prompt_rope[0], private_latent, private_rope,
    )
    out = pl.pallas_call(
        place_kernel,
        out_shape=jax.ShapeDtypeStruct((members, rows, width), bf),
        in_specs=[smem, hbm],
        out_specs=hbm,
        scratch_shapes=[pltpu.VMEM((members, rows, width), bf), dma((members,)), dma((members,))],
    )(src, everything)
    return out.reshape(members, steps, heads, width)


def solution(mesh):
    lead = ("rep", "seq")
    return jax.shard_map(
        per_device,
        mesh=mesh,
        in_specs=(
            P(lead, None, None), P(lead, None, None), P(lead, None, None), P(lead, None, None),
            P(lead), P(lead), P(lead), P(lead),
            P(lead, None, None, None), P(lead, None, None),
        ),
        out_specs=P(lead, None, None, None),
        check_vma=False,
    )
```

```python
import functools
import math

import jax
import jax.numpy as jnp
from jax import lax
from jax.experimental import pallas as pl
from jax.experimental.pallas import tpu as pltpu
from jax.sharding import PartitionSpec as P

DR = 64
NOPE = 128
REACH = 2
TRANSFER_LIMIT = 2
FRESH_ROWS = 16
CHUNKS = 4
MESH = pl.DeviceIdType.MESH
OFFSETS = tuple(o for o in range(-REACH, REACH + 1) if o != 0)
NT = (((1,), (1,)), ((), ()))


def scores_of(q_lat, q_rot, latent, rope):
    s = lax.dot_general(q_lat, latent, NT, preferred_element_type=jnp.float32)
    return s + jnp.dot(q_rot, rope, preferred_element_type=jnp.float32)


def kernel(
    n, heads,
    slot_s, prompt_s, length_s, slot_v, q_hbm, nk_hbm, lat_hbm, rope_hbm, plat_hbm, prope_hbm,
    all_hbm, src_s,
    qin, nkin, lsend, rsend, ksend, lrecv, rrecv, krecv, qg_lat, qg_rot,
    lat, rope, prior_lat, prior_rope, plat, prope,
    m_ref, l_ref, acc_ref, res, osend,
    meta_v, meta_s, rank_s, order_s, qidx_s, osel_s,
    in_sem, meta_send, meta_recv, meta_local, q_send, q_recv, p_send, p_recv, o_send, o_recv, out_sem,
):
    me = lax.axis_index("seq")
    members, rows, width = qin.shape[0], res.shape[1], lat.shape[1]
    rot = rope.shape[0]
    steps = rows // heads
    group = members // 2
    plen = lat.shape[0]
    chunk = plen // CHUNKS
    coef = (NOPE + DR) ** (-0.5) * math.log2(math.e)
    lo = me * members
    peers = [lax.rem(me + o + n, n) for o in OFFSETS]
    nxt = lax.rem(me + 1, n)
    last = len(OFFSETS) - 1

    local = [
        pltpu.make_async_copy(q_hbm, qin, in_sem.at[0]),
        pltpu.make_async_copy(nk_hbm, nkin, in_sem.at[1]),
        pltpu.make_async_copy(plat_hbm, plat, in_sem.at[2]),
        pltpu.make_async_copy(prope_hbm, prope, in_sem.at[3]),
        pltpu.make_async_copy(lat_hbm, lat, in_sem.at[4]),
        pltpu.make_async_copy(rope_hbm, rope, in_sem.at[5]),
    ]
    for c in local:
        c.start()

    barrier = pltpu.get_barrier_semaphore()
    for peer in peers:
        pl.semaphore_signal(barrier, inc=1, device_id={"seq": peer}, device_id_type=MESH)
    pl.semaphore_wait(barrier, len(OFFSETS))

    meta = []
    for k in range(len(OFFSETS)):
        meta.append(pltpu.make_async_remote_copy(
            src_ref=slot_v, dst_ref=meta_v.at[k], send_sem=meta_send.at[k], recv_sem=meta_recv.at[k],
            device_id={"seq": peers[k]}, device_id_type=MESH))
        meta[k].start()

    prompt_copies = []
    for j in range(CHUNKS):
        part = pl.ds(j * chunk, chunk)
        prompt_copies.append((
            pltpu.make_async_remote_copy(
                src_ref=lat_hbm.at[part, :], dst_ref=prior_lat.at[part, :],
                send_sem=p_send.at[2 * j], recv_sem=p_recv.at[2 * j],
                device_id={"seq": nxt}, device_id_type=MESH),
            pltpu.make_async_remote_copy(
                src_ref=rope_hbm.at[:, part], dst_ref=prior_rope.at[:, part],
                send_sem=p_send.at[2 * j + 1], recv_sem=p_recv.at[2 * j + 1],
                device_id={"seq": nxt}, device_id_type=MESH),
        ))
    for c in prompt_copies[0]:
        c.start()

    zero = jnp.int32(0)
    for k in range(len(OFFSETS)):
        meta[k].wait_recv()
    to_smem = pltpu.make_async_copy(meta_v, meta_s, meta_local)
    to_smem.start()
    local[0].wait()
    local[1].wait()
    to_smem.wait()

    def claims(k):
        def step(c, carry):
            count, found = carry
            ns = meta_s[k, 0, c]
            hit = (ns >= lo) & (ns < lo + members)
            found = tuple(
                jnp.where(hit & (count == r), ns - lo, found[r]) for r in range(TRANSFER_LIMIT))
            return count + jnp.where(hit, 1, 0), found
        return lax.fori_loop(0, members, step, (zero, (zero - 1,) * TRANSFER_LIMIT))[1]

    claimed = []
    q_copies = []
    for k in range(len(OFFSETS)):
        found = claims(k)
        claimed.extend(found)
        spots = [jnp.maximum(f, 0) for f in found]
        for r in range(TRANSFER_LIMIT):
            lsend[k, r] = qin[spots[r]][:, :width]
        rsend[k] = jnp.concatenate([qin[at][:, width:] for at in spots], axis=1)
        ksend[k] = functools.reduce(jnp.add, [nkin[at, r] for r, at in enumerate(spots)])
        group_copies = [
            pltpu.make_async_remote_copy(
                src_ref=src.at[k], dst_ref=dst.at[k], send_sem=q_send.at[3 * k + i],
                recv_sem=q_recv.at[3 * k + i],
                device_id={"seq": peers[last - k]}, device_id_type=MESH)
            for i, (src, dst) in enumerate(((lsend, lrecv), (rsend, rrecv), (ksend, krecv)))
        ]
        for c in group_copies:
            c.start()
        q_copies.extend(group_copies)

    def route(c, carry):
        own_count, prior_count, counts, sel = carry
        ns = slot_s[c]
        is_own = jnp.where(prompt_s[c] == me, 1, 0)
        rank = jnp.where(is_own == 1, own_count, group + prior_count)
        rank = jnp.minimum(rank, members - 1)
        rank_s[c] = rank
        place = jnp.where((ns >= lo) & (ns < lo + members), ns - lo, 0)
        counts, sel = list(counts), list(sel)
        for k in range(len(OFFSETS)):
            base = peers[k] * members
            hit = (ns >= base) & (ns < base + members)
            for r in range(TRANSFER_LIMIT):
                this = hit & (counts[k] == r)
                sel[k * TRANSFER_LIMIT + r] = jnp.where(this, rank, sel[k * TRANSFER_LIMIT + r])
                place = jnp.where(this, members + k * TRANSFER_LIMIT + r, place)
            counts[k] = counts[k] + jnp.where(hit, 1, 0)
        qidx_s[c] = place
        return own_count + is_own, prior_count + 1 - is_own, tuple(counts), tuple(sel)

    slots = len(OFFSETS) * TRANSFER_LIMIT
    routed = lax.fori_loop(
        0, members, route, (zero, zero, (zero,) * len(OFFSETS), (zero,) * slots))
    for i in range(slots):
        osel_s[i] = routed[3][i]

    def invert(p, _):
        order_s[p] = lax.fori_loop(
            0, members, lambda c, at: jnp.where(rank_s[c] == p, c, at), zero)
        return 0

    lax.fori_loop(0, members, invert, 0)

    def sources(s, _):
        at = lax.fori_loop(
            0, members, lambda c, v: jnp.where(slot_s[c] == lo + s, rank_s[c], v), zero + members)
        for i in range(slots):
            at = jnp.where(claimed[i] == s, members + 1 + i, at)
        src_s[s] = at
        return 0

    lax.fori_loop(0, members, sources, 0)
    res[members] = jnp.zeros(res.shape[1:], res.dtype)

    for c in q_copies:
        c.wait_send()
    for j in range(1, CHUNKS):
        for c in prompt_copies[j]:
            c.start()
    for c in local[2:]:
        c.wait()
    for c in q_copies:
        c.wait_recv()

    lane = lax.broadcasted_iota(jnp.int32, (rows, plat.shape[1]), 1)
    fresh_col = lax.broadcasted_iota(jnp.int32, (rows, FRESH_ROWS), 1)
    fresh_row = lax.broadcasted_iota(jnp.int32, (rows, FRESH_ROWS), 0)
    first_lane = lane == 0
    share = FRESH_ROWS // TRANSFER_LIMIT

    def begin_one(p):
        c = order_s[p]
        at = qidx_s[c]
        moved = at >= members
        far = jnp.maximum(at - members, 0)
        lane_k, turn = far // TRANSFER_LIMIT, far % TRANSFER_LIMIT
        near = jnp.minimum(at, members - 1)
        home = qin[near]
        q_lat = jnp.where(moved, lrecv[lane_k, turn], home[:, :width])
        packed = rrecv[lane_k]
        far_rot = packed[:, :rot]
        for r in range(1, TRANSFER_LIMIT):
            far_rot = jnp.where(turn == r, packed[:, r * rot:(r + 1) * rot], far_rot)
        q_rot = jnp.where(moved, far_rot, home[:, width:])
        nk = jnp.where(moved, krecv[lane_k], nkin[near, 0])
        base = jnp.where(moved, turn * share, 0)
        block = plat[c]
        s1 = jnp.where(lane < length_s[c], scores_of(q_lat, q_rot, block, prope[c]), -1e30)
        s2 = lax.dot_general(q_lat, nk[:, :width], NT, preferred_element_type=jnp.float32)
        s2 = s2 + lax.dot_general(q_rot, nk[:, width:], NT, preferred_element_type=jnp.float32)
        new = fresh_col - base
        s2 = jnp.where((new >= 0) & (new < steps) & (new * heads <= fresh_row), s2, -1e30)
        top = jnp.maximum(jnp.max(s1, axis=1, keepdims=True), jnp.max(s2, axis=1, keepdims=True))
        w1 = jnp.exp2((s1 - top) * coef)
        w2 = jnp.exp2((s2 - top) * coef)
        total = w1 + jnp.where(first_lane, jnp.sum(w2, axis=1, keepdims=True), 0.0)
        mix = jnp.dot(
            w1.astype(jnp.bfloat16), block, preferred_element_type=jnp.float32
        ) + jnp.dot(w2.astype(jnp.bfloat16), nk[:, :width], preferred_element_type=jnp.float32)
        return q_lat, q_rot, jnp.broadcast_to(top, (rows, m_ref.shape[1])), total, mix

    def begin(b, _):
        made = [begin_one(4 * b + u) for u in range(4)]
        for u in range(4):
            span = pl.ds(pl.multiple_of((4 * b + u) * rows, rows), rows)
            for ref, value in zip((qg_lat, qg_rot, m_ref, l_ref, acc_ref), made[u]):
                ref[span, :] = value
        return 0

    lax.fori_loop(0, members // 4, begin, 0)

    rb = 2 * rows
    lanes = m_ref.shape[1]

    def shared(lat_ref, rope_ref, js, first, final):
        parts = [pl.ds(j * chunk, chunk) for j in js]

        def mixed(b):
            span = pl.ds(pl.multiple_of((first + 2 * b) * rows, rb), rb)
            q_lat, q_rot, before = qg_lat[span, :], qg_rot[span, :], m_ref[span, :]
            tiles = []
            for part in parts:
                s = scores_of(q_lat, q_rot, lat_ref[part, :], rope_ref[:, part])
                tiles.append([s[:, i * lanes:(i + 1) * lanes] for i in range(chunk // lanes)])
            peak = functools.reduce(jnp.maximum, [t for group_ in tiles for t in group_])
            top = jnp.maximum(before, jnp.max(peak, axis=1, keepdims=True))
            fade = jnp.exp2((before - top) * coef)
            total = l_ref[span, :] * fade
            mix = acc_ref[span, :] * jnp.concatenate([fade] * (width // lanes), axis=1)
            for part, group_ in zip(parts, tiles):
                pieces = [jnp.exp2((t - top) * coef) for t in group_]
                total = total + functools.reduce(jnp.add, pieces)
                w = jnp.concatenate([x.astype(jnp.bfloat16) for x in pieces], axis=1)
                mix = mix + jnp.dot(w, lat_ref[part, :], preferred_element_type=jnp.float32)
            return span, top, total, mix

        def step(pair, _):
            made = [mixed(2 * pair + v) for v in range(2)]
            for v in range(2):
                span, top, total, mix = made[v]
                if final:
                    out = (mix * (1.0 / jnp.sum(total, axis=1, keepdims=True))).astype(res.dtype)
                    for u in range(2):
                        res[first + 4 * pair + 2 * v + u] = out[u * rows:(u + 1) * rows]
                else:
                    m_ref[span, :] = top
                    l_ref[span, :] = total
                    acc_ref[span, :] = mix
            return 0

        lax.fori_loop(0, group // 4, step, 0)

    def arrive(js):
        for j in js:
            for c in prompt_copies[j]:
                c.wait_recv()

    shared(lat, rope, range(CHUNKS), 0, True)
    arrive(range(CHUNKS - 1))
    shared(prior_lat, prior_rope, range(CHUNKS - 1), group, False)
    arrive((CHUNKS - 1,))
    shared(prior_lat, prior_rope, (CHUNKS - 1,), group, True)

    o_copies = []
    for k in range(len(OFFSETS)):
        for r in range(TRANSFER_LIMIT):
            osend[k, r] = res[osel_s[k * TRANSFER_LIMIT + r]]
        span = pl.ds(members + 1 + k * TRANSFER_LIMIT, TRANSFER_LIMIT)
        o_copies.append(pltpu.make_async_remote_copy(
            src_ref=osend.at[k], dst_ref=all_hbm.at[span], send_sem=o_send.at[k], recv_sem=o_recv.at[k],
            device_id={"seq": peers[k]}, device_id_type=MESH))
        o_copies[k].start()
    keep = pltpu.make_async_copy(res, all_hbm.at[pl.ds(0, members + 1)], out_sem)
    keep.start()
    for c in meta:
        c.wait_send()
    for pair in prompt_copies:
        for c in pair:
            c.wait_send()
    keep.wait()
    for c in o_copies:
        c.wait()


def place_kernel(src_s, all_hbm, out_hbm, block, in_sem, out_sem):
    members = out_hbm.shape[0]
    reads = [
        pltpu.make_async_copy(all_hbm.at[src_s[s]], block.at[s], in_sem.at[s]) for s in range(members)
    ]
    writes = [
        pltpu.make_async_copy(block.at[s], out_hbm.at[s], out_sem.at[s]) for s in range(members)
    ]
    for c in reads:
        c.start()
    for read, write in zip(reads, writes):
        read.wait()
        write.start()
    for c in writes:
        c.wait()


def per_device(
    prompt_latent, prompt_rope, private_latent, private_rope,
    lengths, survived, prompt_of, new_slot, queries, new_keys,
):
    n = lax.axis_size("seq")
    members, steps, heads, full = queries.shape
    rows = steps * heads
    width = prompt_latent.shape[2]
    plen = prompt_latent.shape[1]
    block = private_latent.shape[1]
    rot = full - width
    kinds = len(OFFSETS)
    slots = kinds * TRANSFER_LIMIT
    share = FRESH_ROWS // TRANSFER_LIMIT
    fresh = jnp.stack([
        jnp.pad(new_keys, ((0, 0), (r * share, FRESH_ROWS - steps - r * share), (0, 0)))
        for r in range(TRANSFER_LIMIT)
    ], axis=1)
    bf, f32, i32 = jnp.bfloat16, jnp.float32, jnp.int32
    smem = pl.BlockSpec(memory_space=pltpu.SMEM)
    hbm = pl.BlockSpec(memory_space=pl.ANY)
    dma = pltpu.SemaphoreType.DMA
    everything, src = pl.pallas_call(
        functools.partial(kernel, n, heads),
        out_shape=(
            jax.ShapeDtypeStruct((members + 1 + slots, rows, width), bf),
            jax.ShapeDtypeStruct((members,), i32)),
        in_specs=[smem, smem, smem, pl.BlockSpec(memory_space=pltpu.VMEM)] + [hbm] * 6,
        out_specs=(hbm, smem),
        scratch_shapes=[
            pltpu.VMEM((members, rows, full), bf),
            pltpu.VMEM((members, TRANSFER_LIMIT, FRESH_ROWS, full), bf),
            pltpu.VMEM((kinds, TRANSFER_LIMIT, rows, width), bf),
            pltpu.VMEM((kinds, rows, TRANSFER_LIMIT * rot), bf),
            pltpu.VMEM((kinds, FRESH_ROWS, full), bf),
            pltpu.VMEM((kinds, TRANSFER_LIMIT, rows, width), bf),
            pltpu.VMEM((kinds, rows, TRANSFER_LIMIT * rot), bf),
            pltpu.VMEM((kinds, FRESH_ROWS, full), bf),
            pltpu.VMEM((members * rows, width), bf),
            pltpu.VMEM((members * rows, rot), bf),
            pltpu.VMEM((plen, width), bf),
            pltpu.VMEM((rot, plen), bf),
            pltpu.VMEM((plen, width), bf),
            pltpu.VMEM((rot, plen), bf),
            pltpu.VMEM((members, block, width), bf),
            pltpu.VMEM((members, rot, block), bf),
            pltpu.VMEM((members * rows, block), f32),
            pltpu.VMEM((members * rows, block), f32),
            pltpu.VMEM((members * rows, width), f32),
            pltpu.VMEM((members + 1, rows, width), bf),
            pltpu.VMEM((kinds, TRANSFER_LIMIT, rows, width), bf),
            pltpu.VMEM((kinds, 1, members), i32),
            pltpu.SMEM((kinds, 1, members), i32),
            pltpu.SMEM((members,), i32),
            pltpu.SMEM((members,), i32),
            pltpu.SMEM((members,), i32),
            pltpu.SMEM((slots,), i32),
            dma((6,)),
            dma((kinds,)),
            dma((kinds,)),
            dma(()),
            dma((3 * kinds,)),
            dma((3 * kinds,)),
            dma((2 * CHUNKS,)),
            dma((2 * CHUNKS,)),
            dma((kinds,)),
            dma((kinds,)),
            dma(()),
        ],
        compiler_params=pltpu.CompilerParams(
            collective_id=0, has_side_effects=True, vmem_limit_bytes=56 * 2**20),
    )(
        new_slot, prompt_of, lengths, new_slot.reshape(1, members),
        queries.reshape(members, rows, full), fresh,
        prompt_latent[0], prompt_rope[0], private_latent, private_rope,
    )
    out = pl.pallas_call(
        place_kernel,
        out_shape=jax.ShapeDtypeStruct((members, rows, width), bf),
        in_specs=[smem, hbm],
        out_specs=hbm,
        scratch_shapes=[pltpu.VMEM((members, rows, width), bf), dma((members,)), dma((members,))],
    )(src, everything)
    return out.reshape(members, steps, heads, width)


def solution(mesh):
    lead = ("rep", "seq")
    return jax.shard_map(
        per_device,
        mesh=mesh,
        in_specs=(
            P(lead, None, None), P(lead, None, None), P(lead, None, None), P(lead, None, None),
            P(lead), P(lead), P(lead), P(lead),
            P(lead, None, None, None), P(lead, None, None),
        ),
        out_specs=P(lead, None, None, None),
        check_vma=False,
    )
```
